128 devices in a mesh: tm: 32 (over y, z_hi, x), pol: 4 (over z_lo, core).
Axes of the slice: x: 4, y: 4, z: 4 (z_hi: 2, z_lo: 2; z = z_hi * 2 + z_lo), core: 2. Of those that a mesh axis runs over, the one named last changes fastest.
Arguments:
- voltages: bfloat16 [128, 1572864], P('pol', 'tm'), may hold values from -22 to 22
- phase_bin: int32 [192], replicated, may hold values from 0 to 7, as said below
Outputs:
- visibilities: bfloat16 [4096, 8, 2, 128, 128], P('tm', None, None, 'pol')
The draws below stay inside these ranges and needn't reach their ends.
Inputs may be any that keep to these rules, and one draw needn't show every extreme that they name: `phase_bin`: each of the 8 bins holds exactly 24 spectra.
All inputs are finite; a program needn't handle non-finite values.
Results may differ from the reference program's by a relative error of at most 0.019.
Values may be sent and summed in bfloat16 or wider, within the bound.
No kernel may reach another device: no remote copies, remote signals or barrier semaphores. Data moves between devices by JAX's collectives and lax.ppermute only.
A program may use at most 320 MiB of HBM per device.

```python
import math
import jax
import jax.numpy as jnp
from jax import lax

PATHS = 128
FFT_LEN = 8192
TAPS = 4
NBINS = 8
CHANNELS = 4096
SPECTRA = 192
SAMPLES = 1572864


def draw_voltages(key, part):
    key = jax.random.fold_in(key, 11)
    noise_key, scale_key = jax.random.split(key, 2)
    place = jnp.arange(SAMPLES, dtype=jnp.float32) / SAMPLES
    block_scale = jnp.exp(0.5 * math.log(10.0) * jax.random.uniform(scale_key, (PATHS, SPECTRA)))
    block_scale = jnp.repeat(block_scale, FFT_LEN, axis=1)
    noise = jnp.clip(jax.random.normal(noise_key, (PATHS, SAMPLES)), -4.0, 4.0)
    envelope = jnp.sqrt(1.0 + 2.0 * place)
    return (noise * envelope[None, :] * block_scale).astype(jnp.bfloat16)


def draw_phase_bin(key, part):
    key = jax.random.fold_in(key, 5)
    labels = jnp.arange(SPECTRA, dtype=jnp.int32) % NBINS
    return jax.random.permutation(key, labels).astype(jnp.int32)


def setup_inputs(seed: int = 0) -> dict:
    splits = jax.random.split(jax.random.key(seed), 3)
    voltages = draw_voltages(jax.random.fold_in(splits[2], 71), 0)
    phase_bin = draw_phase_bin(jax.random.fold_in(splits[2], 71), 0)
    return {"voltages": voltages, "phase_bin": phase_bin}


def filter_window():
    length = TAPS * FFT_LEN
    place = jnp.arange(length, dtype=jnp.float32)
    center = (place - length / 2 + 0.5) / FFT_LEN
    taper = 0.5 - 0.5 * jnp.cos(2.0 * math.pi * (place + 0.5) / length)
    return (jnp.sinc(center) * taper).reshape(TAPS, FFT_LEN)

def dft_table(first, count):
    samples = jnp.arange(FFT_LEN, dtype=jnp.int32)
    columns = first + jnp.arange(count, dtype=jnp.int32)
    phase = samples[:, None] * columns[None, :] % FFT_LEN
    angle = phase.astype(jnp.float32) * (2.0 * math.pi / FFT_LEN)
    return jnp.concatenate([jnp.cos(angle), -jnp.sin(angle)], axis=1).astype(jnp.bfloat16)

def transform(spectra_rows):
    block_width = min(512, CHANNELS)
    real_parts = []
    imag_parts = []
    for number in range(CHANNELS // block_width):
        table = dft_table(number * block_width, block_width)
        product = jnp.dot(spectra_rows, table, preferred_element_type=jnp.float32)
        real_parts.append(product[:, :block_width])
        imag_parts.append(product[:, block_width:])
    return (jnp.concatenate(real_parts, axis=1), jnp.concatenate(imag_parts, axis=1))

def bin_grams(ordered):
    per_bin = SPECTRA // NBINS
    width = ordered.shape[-1]
    grouped = ordered.astype(jnp.float32).reshape(2, NBINS, per_bin, PATHS, width)
    left_side = jnp.concatenate([grouped[0], grouped[1]], axis=1)
    right_imag = jnp.concatenate([-grouped[1], grouped[0]], axis=1)
    real_sum = jnp.einsum('bsic,bsjc->cbij', left_side, left_side)
    imag_sum = jnp.einsum('bsic,bsjc->cbij', left_side, right_imag)
    return (jnp.stack([real_sum, imag_sum], axis=2) / per_bin).astype(jnp.bfloat16)

def reference(voltages, phase_bin):
    blocks = voltages.reshape(PATHS, SPECTRA, FFT_LEN)
    padded = jnp.concatenate([jnp.zeros((PATHS, TAPS - 1, FFT_LEN), voltages.dtype), blocks], axis=1)
    window = filter_window()
    filtered = jnp.zeros((PATHS, SPECTRA, FFT_LEN), jnp.float32)
    for tap in range(TAPS):
        filtered = filtered + window[tap] * padded[:, tap:tap + SPECTRA].astype(jnp.float32)
    filtered = filtered.astype(jnp.bfloat16)
    spectra_rows = jnp.transpose(filtered, (1, 0, 2)).reshape(SPECTRA * PATHS, FFT_LEN)
    real_part, imag_part = transform(spectra_rows)
    real_part = real_part.reshape(SPECTRA, PATHS, CHANNELS)
    imag_part = imag_part.reshape(SPECTRA, PATHS, CHANNELS)
    bandpass = lax.optimization_barrier(jnp.sum(real_part * real_part + imag_part * imag_part, axis=0))
    equalizer = lax.rsqrt(bandpass / SPECTRA + 1e-06)
    scaled = jnp.stack([real_part * equalizer, imag_part * equalizer]).astype(jnp.bfloat16)
    ordering = jnp.argsort(phase_bin, stable=True).astype(jnp.int32)
    ordered = jnp.take(scaled, ordering, axis=1)
    chan_block = min(128, CHANNELS)
    count = CHANNELS // chan_block
    grouped = ordered.reshape(2, SPECTRA, PATHS, count, chan_block).transpose(3, 0, 1, 2, 4)
    result = lax.map(bin_grams, grouped)
    return result.reshape(CHANNELS, NBINS, 2, PATHS, PATHS)
```

```python
import functools
import math

import jax
import jax.numpy as jnp
import ml_dtypes
import numpy as np
from jax import lax
from jax.experimental import pallas as pl
from jax.experimental.pallas import tpu as pltpu
from jax.sharding import PartitionSpec as P

FFT_LEN = 8192
TAPS = 4
NBINS = 8
CHANNELS = 4096
RADIX = 8
INNER = FFT_LEN // RADIX
LANES = 128
HALF = 3
NT = (((1,), (1,)), ((), ()))


def filter_window():
    length = TAPS * FFT_LEN
    place = np.arange(length, dtype=np.float64)
    center = (place - length / 2 + 0.5) / FFT_LEN
    taper = 0.5 - 0.5 * np.cos(2.0 * math.pi * (place + 0.5) / length)
    return (np.sinc(center) * taper).reshape(TAPS, FFT_LEN).astype(np.float32)


def twiddles():
    angle = 2.0 * math.pi * np.outer(np.arange(RADIX), np.arange(INNER)) / FFT_LEN
    return np.concatenate([np.cos(angle), np.sin(angle)]).astype(np.float32)


def inner_table(time_devs):
    angle = 2.0 * math.pi * (np.outer(np.arange(INNER // 2), np.arange(INNER)) % INNER) / INNER
    real_rows = np.concatenate([np.cos(angle), np.sin(angle)], axis=1)
    imag_rows = np.concatenate([-np.sin(angle), np.cos(angle)], axis=1)
    rows = np.stack([part.reshape(time_devs, -1, 2 * INNER) for part in (real_rows, imag_rows)], axis=1)
    return rows.reshape(INNER, 2 * INNER).astype(ml_dtypes.bfloat16)


def spectra_kernel(first_ref, second_ref, window_ref, twiddle_ref, table_ref, out_ref, z_ref):
    paths = first_ref.shape[0]
    root = math.sqrt(0.5)

    def block(lane, carry):
        for s in range(HALF):
            f = []
            for n1 in range(RADIX):
                total = None
                for tap in range(TAPS):
                    number = s + tap
                    source = first_ref if number < HALF else second_ref
                    start = (number % HALF) * FFT_LEN + n1 * INNER
                    at = pl.ds(pl.multiple_of(start + lane * LANES, LANES), LANES)
                    w_at = pl.ds(pl.multiple_of(n1 * INNER + lane * LANES, LANES), LANES)
                    term = window_ref[tap : tap + 1, w_at] * source[:, at].astype(jnp.float32)
                    total = term if total is None else total + term
                f.append(total.astype(jnp.bfloat16).astype(jnp.float32))
            a = [f[n] + f[n + 4] for n in range(4)]
            b = [f[n] - f[n + 4] for n in range(4)]
            low, high = root * (b[1] - b[3]), root * (b[1] + b[3])
            y1 = (b[0] + low, -b[2] - high)
            y3 = (b[0] - low, b[2] - high)
            y2 = (a[0] - a[2], a[3] - a[1])
            even, odd = a[0] + a[2], a[1] + a[3]
            y = [(even + odd, None), y1, y2, y3, (even - odd, None)]
            y += [(re, -im) for re, im in (y3, y2, y1)]
            for k1 in range(RADIX):
                re, im = y[k1]
                at = pl.ds(pl.multiple_of(lane * LANES, LANES), LANES)
                if k1 == 0:
                    z_re, z_im = re, jnp.zeros_like(re)
                else:
                    cos = twiddle_ref[k1 : k1 + 1, at]
                    sin = twiddle_ref[RADIX + k1 : RADIX + k1 + 1, at]
                    if im is None:
                        z_re, z_im = re * cos, -re * sin
                    else:
                        z_re, z_im = re * cos + im * sin, im * cos - re * sin
                row = ((k1 // 4) * HALF + s) * 4 * paths + (k1 % 4) * paths
                z_ref[row : row + paths, at] = z_re.astype(jnp.bfloat16)
                at = pl.ds(pl.multiple_of(INNER + lane * LANES, LANES), LANES)
                z_ref[row : row + paths, at] = z_im.astype(jnp.bfloat16)
        return carry

    lax.fori_loop(0, INNER // LANES, block, 0)

    rows = 256

    def product(number, carry):
        at = pl.ds(pl.multiple_of(number * rows, rows), rows)
        out_ref[at, :] = lax.dot_general(
            table_ref[at, :], z_ref[...], NT, preferred_element_type=jnp.float32
        ).astype(jnp.bfloat16)
        return carry

    lax.fori_loop(0, INNER // rows, product, 0)


def spectra(first, first_at, second, second_at, window, twiddle, table):
    paths = first.shape[0]
    width = HALF * FFT_LEN
    lanes = RADIX * HALF * paths
    return pl.pallas_call(
        spectra_kernel,
        grid=(1,),
        out_shape=jax.ShapeDtypeStruct((INNER, lanes), jnp.bfloat16),
        in_specs=[
            pl.BlockSpec((paths, width), lambda i: (0, first_at)),
            pl.BlockSpec((paths, width), lambda i: (0, second_at)),
            pl.BlockSpec(window.shape, lambda i: (0, 0)),
            pl.BlockSpec(twiddle.shape, lambda i: (0, 0)),
            pl.BlockSpec(table.shape, lambda i: (0, 0)),
        ],
        out_specs=pl.BlockSpec((INNER, lanes), lambda i: (0, 0)),
        scratch_shapes=[pltpu.VMEM((lanes, 2 * INNER), jnp.bfloat16)],
        compiler_params=pltpu.CompilerParams(vmem_limit_bytes=48 * 1024 * 1024),
        cost_estimate=pl.CostEstimate(
            flops=2 * INNER * 2 * INNER * lanes, bytes_accessed=9 * 2**20, transcendentals=0
        ),
        name="spectra",
    )(first, second, window, twiddle, table)


def gram_kernel(per_bin, *refs):
    parts = (refs[0:4], refs[4:8])
    place_ref, own_ref, mask_ref, out_ref, g_ref = refs[8:]
    times, rows, _ = parts[0][0].shape
    chans = rows // 2
    group = 8

    @pl.when(pl.program_id(1) == 0)
    def _():
        def regroup(number, carry):
            t_at = pl.ds(number * group, group)
            at = pl.ds(pl.multiple_of(number * group * rows, group * rows), group * rows)
            for half, sources in enumerate(parts):
                for s in range(HALF):
                    lanes = slice(s * LANES, (s + 1) * LANES)
                    left = jnp.concatenate(
                        [r[t_at, :, lanes].reshape(group * rows, LANES) for r in sources], axis=1
                    )
                    moved = jnp.dot(left, place_ref[...], preferred_element_type=jnp.float32)
                    for low in range(4):
                        g_ref[half * HALF + s, low, at, :] = moved[:, low * LANES : (low + 1) * LANES]
            return carry

        lax.fori_loop(0, times // group, regroup, 0)

    per_step = out_ref.shape[0]
    total = times * 2 * HALF
    for step in range(per_step):
        chan = pl.program_id(1) * per_step + step
        for low in range(4):
            re = jnp.concatenate(
                [g_ref[s, low, pl.ds(chan, times, stride=rows), :] for s in range(2 * HALF)], axis=0
            )
            im = jnp.concatenate(
                [g_ref[s, low, pl.ds(chans + chan, times, stride=rows), :] for s in range(2 * HALF)], axis=0
            )
            power = jnp.sum(re * re + im * im, axis=0, keepdims=True)
            equalizer = lax.rsqrt(power / total + 1e-06)
            re = (re * equalizer).astype(jnp.bfloat16)
            im = (im * equalizer).astype(jnp.bfloat16)
            both = jnp.concatenate([re, im], axis=0)
            turned = jnp.concatenate([-im, re], axis=0)
            left = lax.dot_general(own_ref[...], both, NT, preferred_element_type=jnp.float32)
            left = jnp.concatenate([left.astype(jnp.bfloat16)] * NBINS, axis=0) * mask_ref[...]
            right = jnp.concatenate([both, turned], axis=1)
            result = jnp.dot(left, right, preferred_element_type=jnp.float32) * (1.0 / per_bin)
            result = result.astype(jnp.bfloat16)
            shape = (NBINS, own_ref.shape[0], LANES)
            out_ref[step, 0, low, :, 0] = result[:, :LANES].reshape(shape)
            out_ref[step, 0, low, :, 1] = result[:, LANES:].reshape(shape)


def grams(early, late, place, own, mask, per_bin):
    times, rows, lanes = early[0].shape
    chans = rows // 2
    paths = own.shape[0]
    per_step = 2
    block = pl.BlockSpec((times, rows, lanes // 2), lambda i, j: (0, 0, i))
    return pl.pallas_call(
        functools.partial(gram_kernel, per_bin),
        grid=(2, chans // per_step),
        out_shape=jax.ShapeDtypeStruct((chans, 2, 4, NBINS, 2, paths, LANES), jnp.bfloat16),
        in_specs=[block] * 8
        + [
            pl.BlockSpec(place.shape, lambda i, j: (0, 0)),
            pl.BlockSpec(own.shape, lambda i, j: (0, 0)),
            pl.BlockSpec(mask.shape, lambda i, j: (0, 0)),
        ],
        out_specs=pl.BlockSpec(
            (per_step, 1, 4, NBINS, 2, paths, LANES), lambda i, j: (j, i, 0, 0, 0, 0, 0)
        ),
        scratch_shapes=[pltpu.VMEM((2 * HALF, 4, times * rows, LANES), jnp.float32)],
        compiler_params=pltpu.CompilerParams(vmem_limit_bytes=48 * 1024 * 1024),
        cost_estimate=pl.CostEstimate(
            flops=9 * 2**30, bytes_accessed=30 * 2**20, transcendentals=0
        ),
        name="grams",
    )(*early, *late, place, own, mask)


def swapped(x, by):
    return lax.ppermute(x, "pol", [(i, i ^ by) for i in range(4)])


def on_device(voltages, phase_bin):
    paths, samples = voltages.shape
    time_devs = lax.axis_size("tm")
    path_devs = lax.axis_size("pol")
    total = time_devs * 2 * HALF
    width = HALF * FFT_LEN
    halo = lax.ppermute(
        voltages[:, samples - width :], "tm", [(i, i + 1) for i in range(time_devs - 1)]
    )
    window = jnp.asarray(filter_window())
    twiddle = jnp.asarray(twiddles())
    table = jnp.asarray(inner_table(time_devs))

    me = lax.axis_index("pol")
    src = jnp.arange(4 * LANES, dtype=jnp.int32)[:, None]
    dst = jnp.arange(4 * LANES, dtype=jnp.int32)[None, :]
    device = jnp.bitwise_xor(src // LANES, me)
    target = (src % LANES) // paths * LANES + device * paths + src % paths
    place = (target == dst).astype(jnp.bfloat16)
    own = (
        jnp.arange(paths, dtype=jnp.int32)[:, None] + me * paths
        == jnp.arange(LANES, dtype=jnp.int32)[None, :]
    ).astype(jnp.bfloat16)
    labels = phase_bin.reshape(time_devs, 2, HALF)
    labels = jnp.concatenate([labels[:, 1].T.reshape(-1), labels[:, 0].T.reshape(-1)])
    mask = labels[None, :] == jnp.arange(NBINS, dtype=jnp.int32)[:, None]
    mask = jnp.repeat(jnp.concatenate([mask, mask], axis=1), paths, axis=0).astype(jnp.bfloat16)

    def exchanged(x):
        x = x.reshape(time_devs, INNER // time_devs, -1)
        return lax.all_to_all(x, "tm", split_axis=0, concat_axis=0, tiled=True)

    late = exchanged(spectra(voltages, 0, voltages, 1, window, twiddle, table))
    late_z = swapped(late, 2)
    early = exchanged(spectra(halo, 0, voltages, 0, window, twiddle, table))
    early_z = swapped(early, 2)
    late = (late, swapped(late, 1), late_z, swapped(late_z, 1))
    early = (early, swapped(early, 1), early_z, swapped(early_z, 1))
    out = grams(late, early, place, own, mask, total // NBINS)
    return out.reshape(CHANNELS // time_devs, NBINS, 2, paths, paths * path_devs)


def solution(mesh):
    in_specs = (P("pol", "tm"), P())
    out_specs = P("tm", None, None, "pol", None)
    return jax.shard_map(
        on_device, mesh=mesh, in_specs=in_specs, out_specs=out_specs, check_vma=False
    )
```

```python
import functools
import math

import jax
import jax.numpy as jnp
import ml_dtypes
import numpy as np
from jax import lax
from jax.experimental import pallas as pl
from jax.experimental.pallas import tpu as pltpu
from jax.sharding import PartitionSpec as P

FFT_LEN = 8192
TAPS = 4
NBINS = 8
CHANNELS = 4096
RADIX = 16
INNER = FFT_LEN // RADIX
LANES = 128
HALF = 3
NT = (((1,), (1,)), ((), ()))


def filter_window():
    length = TAPS * FFT_LEN
    place = np.arange(length, dtype=np.float64)
    center = (place - length / 2 + 0.5) / FFT_LEN
    taper = 0.5 - 0.5 * np.cos(2.0 * math.pi * (place + 0.5) / length)
    return (np.sinc(center) * taper).reshape(TAPS, FFT_LEN).astype(np.float32)


def twiddles():
    angle = 2.0 * math.pi * np.outer(np.arange(RADIX), np.arange(INNER)) / FFT_LEN
    return np.concatenate([np.cos(angle), np.sin(angle)]).astype(np.float32)


def inner_table(time_devs):
    angle = 2.0 * math.pi * (np.outer(np.arange(INNER // 2), np.arange(INNER)) % INNER) / INNER
    real_rows = np.concatenate([np.cos(angle), np.sin(angle)], axis=1)
    imag_rows = np.concatenate([-np.sin(angle), np.cos(angle)], axis=1)
    rows = np.stack([part.reshape(time_devs, -1, 2 * INNER) for part in (real_rows, imag_rows)], axis=1)
    rows = rows.reshape(4, 2, 4, -1).transpose(1, 0, 2, 3)
    return rows.reshape(INNER, 2 * INNER).astype(ml_dtypes.bfloat16)


def real_transform8(f):
    root = math.sqrt(0.5)
    a = [f[n] + f[n + 4] for n in range(4)]
    b = [f[n] - f[n + 4] for n in range(4)]
    low, high = root * (b[1] - b[3]), root * (b[1] + b[3])
    even, odd = a[0] + a[2], a[1] + a[3]
    return [
        (even + odd, None),
        (b[0] + low, -b[2] - high),
        (a[0] - a[2], a[3] - a[1]),
        (b[0] - low, b[2] - high),
        (even - odd, None),
    ]


def real_transform16(f):
    e = real_transform8(f[0::2])
    o = real_transform8(f[1::2])
    y = [None] * 9
    y[0] = (e[0][0] + o[0][0], None)
    y[8] = (e[0][0] - o[0][0], None)
    y[4] = (e[4][0], -o[4][0])
    for k in range(1, 4):
        cos, sin = math.cos(math.pi * k / 8), math.sin(math.pi * k / 8)
        re = o[k][0] * cos + o[k][1] * sin
        im = o[k][1] * cos - o[k][0] * sin
        y[k] = (e[k][0] + re, e[k][1] + im)
        y[8 - k] = (e[k][0] - re, im - e[k][1])
    return y


def spectra_kernel(first_ref, second_ref, window_ref, twiddle_ref, table_ref, side_ref, *refs):
    out_refs, z_ref = refs[:-1], refs[-1]
    paths = first_ref.shape[0]
    strip = 16

    def block(lane, carry):
        for s in range(HALF):
            for top in range(0, paths, strip):
                f = []
                for n1 in range(RADIX):
                    total = None
                    for tap in range(TAPS):
                        number = s + tap
                        source = first_ref if number < HALF else second_ref
                        start = number % HALF * FFT_LEN + n1 * INNER
                        at = pl.ds(pl.multiple_of(start + lane * LANES, LANES), LANES)
                        w_at = pl.ds(pl.multiple_of(n1 * INNER + lane * LANES, LANES), LANES)
                        volts = source[top : top + strip, at].astype(jnp.float32)
                        term = window_ref[tap : tap + 1, w_at] * volts
                        total = term if total is None else total + term
                    f.append(total.astype(jnp.bfloat16).astype(jnp.float32))
                y = real_transform16(f)
                re_at = pl.ds(pl.multiple_of(lane * LANES, LANES), LANES)
                im_at = pl.ds(pl.multiple_of(INNER + lane * LANES, LANES), LANES)
                for k1 in range(RADIX):
                    re, im = y[min(k1, RADIX - k1)]
                    if k1 > RADIX - k1:
                        im = -im
                    if k1 == 0:
                        z_re, z_im = re, jnp.zeros_like(re)
                    else:
                        cos = twiddle_ref[k1 : k1 + 1, re_at]
                        sin = twiddle_ref[RADIX + k1 : RADIX + k1 + 1, re_at]
                        if im is None:
                            z_re, z_im = re * cos, -re * sin
                        else:
                            z_re, z_im = re * cos + im * sin, im * cos - re * sin
                    row = ((k1 // 4) * HALF + s) * 4 * paths + (k1 % 4) * paths + top
                    z_ref[row : row + strip, re_at] = z_re.astype(jnp.bfloat16)
                    z_ref[row : row + strip, im_at] = z_im.astype(jnp.bfloat16)
        return carry

    lax.fori_loop(0, INNER // LANES, block, 0)

    rows = INNER // 2

    def product(number, carry):
        at = pl.ds(pl.multiple_of((number ^ side_ref[0]) * rows, rows), rows)
        result = lax.dot_general(
            table_ref[at, :], z_ref[...], NT, preferred_element_type=jnp.float32
        ).astype(jnp.bfloat16)

        for part, ref in enumerate(out_refs):
            @pl.when(number == part)
            def _():
                ref[...] = result

        return carry

    lax.fori_loop(0, 2, product, 0)


def spectra(first, second, second_at, window, twiddle, table, side):
    paths = first.shape[0]
    lanes = RADIX * HALF * paths
    out = jax.ShapeDtypeStruct((INNER // 2, lanes), jnp.bfloat16)
    return pl.pallas_call(
        spectra_kernel,
        grid=(1,),
        out_shape=[out] * 2,
        in_specs=[
            pl.BlockSpec((paths, HALF * FFT_LEN), lambda i: (0, 0)),
            pl.BlockSpec((paths, HALF * FFT_LEN), lambda i: (0, second_at)),
            pl.BlockSpec(window.shape, lambda i: (0, 0)),
            pl.BlockSpec(twiddle.shape, lambda i: (0, 0)),
            pl.BlockSpec(table.shape, lambda i: (0, 0)),
            pl.BlockSpec(memory_space=pltpu.SMEM),
        ],
        out_specs=[pl.BlockSpec(out.shape, lambda i: (0, 0))] * 2,
        scratch_shapes=[pltpu.VMEM((lanes, 2 * INNER), jnp.bfloat16)],
        compiler_params=pltpu.CompilerParams(vmem_limit_bytes=48 * 1024 * 1024),
        cost_estimate=pl.CostEstimate(
            flops=2**20, bytes_accessed=2**20, transcendentals=0
        ),
        name="spectra",
    )(first, second, window, twiddle, table, side)


def gram_kernel(*refs):
    parts = [refs[4 * n : 4 * n + 4] for n in range(4)]
    place_ref, own_ref, mask_ref, rank_ref = refs[16:20]
    out_ref, g_ref, o_ref = refs[-3:]
    times, rows, width = parts[0][0].shape
    chans = rows // 2
    total = 4 * HALF * times
    groups = width // (HALF * LANES)

    @pl.when(pl.program_id(0) == 0)
    def _():
        def regroup(number, carry):
            s = lax.rem(number, HALF)
            low = number // HALF * 4
            lanes = pl.ds(pl.multiple_of(number * LANES, LANES), LANES)
            left = jnp.concatenate(
                [
                    jnp.concatenate([r[:, :, lanes].reshape(times * rows, LANES) for r in sources], axis=1)
                    for sources in parts
                ],
                axis=0,
            )
            moved = jnp.dot(left, place_ref[...], preferred_element_type=jnp.float32)
            mine = left[:, :LANES].astype(jnp.float32)
            for n in range(len(parts)):
                for t in range(times):
                    rank = rank_ref[(n * HALF + s) * times + t]
                    at = pl.ds(pl.multiple_of(rank * rows, rows), rows)
                    here = slice((n * times + t) * rows, (n * times + t + 1) * rows)
                    o_ref[number // HALF, at, :] = mine[here]
                    for l in range(4):
                        g_ref[low + l, at, :] = moved[here, l * LANES : (l + 1) * LANES]
            return carry

        lax.fori_loop(0, groups * HALF, regroup, 0)

    chan = pl.program_id(0)
    side = total // 2
    paths = LANES // 4
    shape = (NBINS // 2, paths, LANES)

    def scaled(ref, low):
        re = ref[low, pl.ds(chan, total, stride=rows), :]
        im = ref[low, pl.ds(chans + chan, total, stride=rows), :]
        power = jnp.sum(re * re + im * im, axis=0, keepdims=True)
        equalizer = lax.rsqrt(power / total + 1e-06) * math.sqrt(NBINS / total)
        return (re * equalizer).astype(jnp.bfloat16), (im * equalizer).astype(jnp.bfloat16)

    halves = [slice(half * side, (half + 1) * side) for half in range(2)]
    for group in range(groups):
        re, im = scaled(o_ref, group)
        turned_own = [
            lax.dot_general(
                own_ref[...], jnp.concatenate([re[at], im[at]], axis=0), NT, preferred_element_type=jnp.float32
            ).astype(jnp.bfloat16)
            for at in halves
        ]
        for l in range(4):
            low = group * 4 + l
            re, im = scaled(g_ref, low)
            for half, at in enumerate(halves):
                left = turned_own[half][l * paths : (l + 1) * paths]
                left = jnp.concatenate([left] * (NBINS // 2), axis=0) * mask_ref[...]
                both = jnp.concatenate([re[at], im[at]], axis=0)
                turned = jnp.concatenate([-im[at], re[at]], axis=0)
                right = jnp.concatenate([both, turned], axis=1)
                result = jnp.dot(left, right, preferred_element_type=jnp.float32).astype(jnp.bfloat16)
                bins = slice(half * NBINS // 2, (half + 1) * NBINS // 2)
                out_ref[0, low, bins, 0] = result[:, :LANES].reshape(shape)
                out_ref[0, low, bins, 1] = result[:, LANES:].reshape(shape)


def grams(sources, place, own, mask, rank, part, before):
    times, rows, _ = sources[0].shape
    chans = rows // 2
    paths = own.shape[0] // 4
    lanes = RADIX // 2 * HALF * paths
    lows = RADIX // 2

    def block(x):
        at = part if x.shape[2] > lanes else 0
        return pl.BlockSpec((times, rows, lanes), lambda j: (0, 0, at))

    args = (*sources, place, own, mask, rank)
    in_specs = [block(x) for x in sources] + [
        pl.BlockSpec(place.shape, lambda j: (0, 0)),
        pl.BlockSpec(own.shape, lambda j: (0, 0)),
        pl.BlockSpec(mask.shape, lambda j: (0, 0)),
        pl.BlockSpec(memory_space=pltpu.SMEM),
    ]
    aliases = {}
    if before is not None:
        aliases = {len(args): 0}
        args += (before,)
        in_specs.append(pl.BlockSpec(memory_space=pl.ANY))
    return pl.pallas_call(
        gram_kernel,
        grid=(chans,),
        out_shape=jax.ShapeDtypeStruct((chans, RADIX, NBINS, 2, paths, LANES), jnp.bfloat16),
        in_specs=in_specs,
        out_specs=pl.BlockSpec((1, lows, NBINS, 2, paths, LANES), lambda j: (j, part, 0, 0, 0, 0)),
        scratch_shapes=[
            pltpu.VMEM((lows, rank.shape[0] * rows, LANES), jnp.float32),
            pltpu.VMEM((lows // 4, rank.shape[0] * rows, LANES), jnp.float32),
        ],
        input_output_aliases=aliases,
        compiler_params=pltpu.CompilerParams(vmem_limit_bytes=48 * 1024 * 1024),
        cost_estimate=pl.CostEstimate(flops=9 * 2**29, bytes_accessed=15 * 2**20, transcendentals=0),
        name="grams",
    )(*args)


def follows(x, *others):
    return pl.pallas_call(
        lambda *refs: None,
        out_shape=jax.ShapeDtypeStruct(x.shape, x.dtype),
        in_specs=[pl.BlockSpec(memory_space=pl.ANY)] * (1 + len(others)),
        out_specs=pl.BlockSpec(memory_space=pl.ANY),
        input_output_aliases={0: 0},
        cost_estimate=pl.CostEstimate(flops=0, bytes_accessed=0, transcendentals=0),
        name="follows",
    )(x, *others)


def swapped(x, by):
    return lax.ppermute(x, "pol", [(i, i ^ by) for i in range(4)])


def on_device(voltages, phase_bin):
    paths, samples = voltages.shape
    time_devs = lax.axis_size("tm")
    path_devs = lax.axis_size("pol")
    total = time_devs * 2 * HALF
    width = HALF * FFT_LEN
    pairs = [(i, i + 1) for i in range(time_devs - 1)]
    halo = lax.ppermute(voltages[:, samples - width :], "tm", pairs)
    window = jnp.asarray(filter_window())
    twiddle = jnp.asarray(twiddles())
    table = jnp.asarray(inner_table(time_devs))

    me = lax.axis_index("pol")
    src = jnp.arange(4 * LANES, dtype=jnp.int32)[:, None]
    dst = jnp.arange(4 * LANES, dtype=jnp.int32)[None, :]
    device = jnp.bitwise_xor(src // LANES, me)
    target = (src % LANES) // paths * LANES + device * paths + src % paths
    place = (target == dst).astype(jnp.bfloat16)
    own = jnp.eye(LANES, dtype=jnp.bfloat16)
    t_at = lax.axis_index("tm")
    side = t_at // 4 % 2
    labels = phase_bin.reshape(4, 2, 4, 2, HALF)
    labels = jnp.where(side == 0, labels, labels[:, ::-1])[:, :, :, ::-1]
    labels = labels.transpose(3, 1, 4, 0, 2).reshape(-1)
    number = jnp.arange(total, dtype=jnp.int32)
    ahead = (labels[:, None] == labels[None, :]) & (number[:, None] > number[None, :])
    rank = labels * (total // NBINS) + jnp.sum(ahead.astype(jnp.int32), axis=1)
    rank = jnp.clip(rank, 0, total - 1)
    mask = np.arange(NBINS // 2)[:, None] == np.arange(total // 2)[None, :] // (total // NBINS)
    mask = jnp.asarray(np.repeat(np.tile(mask, (1, 2)), paths, axis=0).astype(ml_dtypes.bfloat16))

    groups = [[y * 8 + z * 4 + x for y in range(4) for x in range(4)] for z in range(2)]
    across = []
    for t in range(time_devs):
        for q in range(path_devs):
            across.append((t * path_devs + q, (t ^ 4) * path_devs + (q ^ 2)))

    def exchanged(x):
        x = x.reshape(time_devs // 2, INNER // time_devs, -1)
        return lax.all_to_all(
            x, "tm", split_axis=0, concat_axis=0, axis_index_groups=groups, tiled=True
        )

    def crossed(x):
        return lax.ppermute(x, ("tm", "pol"), across)

    def after(x, *others):
        return lax.optimization_barrier((x, *others))[0]

    def own_set(x, z):
        return (x, swapped(x, 1), z, swapped(z, 1))

    def cross_set(x, z):
        return (z, swapped(z, 1), x, swapped(x, 1))

    side = side.reshape(1).astype(jnp.int32)
    late, late_x = spectra(voltages, voltages, 1, window, twiddle, table, side)
    late_x = crossed(late_x)
    late = exchanged(late)
    late_z = swapped(late, 2)
    late_c = swapped(late, 1)
    late_x = exchanged(after(late_x, late))
    halo = after(halo, late_x)
    early, early_x = spectra(halo, voltages, 0, window, twiddle, table, side)
    late_xz = swapped(late_x, 2)
    late_xc = swapped(late_x, 1)
    late_zc = swapped(late_z, 1)
    early_x = crossed(early_x)
    early = exchanged(after(early, late_z))
    early_z = swapped(early, 2)
    early_x = exchanged(after(early_x, early, late_xz, late_c, late_xc, late_zc))
    half = early_x.shape[2] // 2
    low_z = swapped(after(early_x[:, :, :half], early_z), 2)
    late_xzc = swapped(late_xz, 1)
    early_c = swapped(early, 1)
    early_zc = swapped(early_z, 1)
    early_xc = swapped(early_x, 1)
    high_z = swapped(after(early_x[:, :, half:], low_z), 2)
    common = (late, late_c, late_z, late_zc, late_xz, late_xzc, late_x, late_xc)
    common += (early, early_c, early_z, early_zc)
    low = (low_z, swapped(low_z, 1), early_x, early_xc)
    out = grams(common + low, place, own, mask, rank, 0, None)
    high_z = follows(high_z, out)
    high = (high_z, swapped(high_z, 1), early_x, early_xc)
    out = grams(common + high, place, own, mask, rank, 1, out)
    return out.reshape(CHANNELS // time_devs, NBINS, 2, paths, paths * path_devs)


def solution(mesh):
    in_specs = (P("pol", "tm"), P())
    out_specs = P("tm", None, None, "pol", None)
    return jax.shard_map(
        on_device, mesh=mesh, in_specs=in_specs, out_specs=out_specs, check_vma=False
    )
```

```python
import functools
import math

import jax
import jax.numpy as jnp
import ml_dtypes
import numpy as np
from jax import lax
from jax.experimental import pallas as pl
from jax.experimental.pallas import tpu as pltpu
from jax.sharding import PartitionSpec as P

FFT_LEN = 8192
TAPS = 4
NBINS = 8
CHANNELS = 4096
RADIX = 16
INNER = FFT_LEN // RADIX
LANES = 128
VMEM_BYTES = 60 * 1024 * 1024
HALF = 3
NT = (((1,), (1,)), ((), ()))


def filter_window():
    length = TAPS * FFT_LEN
    place = np.arange(length, dtype=np.float64)
    center = (place - length / 2 + 0.5) / FFT_LEN
    taper = 0.5 - 0.5 * np.cos(2.0 * math.pi * (place + 0.5) / length)
    return (np.sinc(center) * taper).reshape(TAPS, FFT_LEN).astype(np.float32)


def twiddles():
    angle = 2.0 * math.pi * np.outer(np.arange(RADIX), np.arange(INNER)) / FFT_LEN
    return np.concatenate([np.cos(angle), np.sin(angle)]).astype(np.float32)


def inner_table(time_devs):
    angle = 2.0 * math.pi * (np.outer(np.arange(INNER // 2), np.arange(INNER)) % INNER) / INNER
    real_rows = np.concatenate([np.cos(angle), np.sin(angle)], axis=1)
    imag_rows = np.concatenate([-np.sin(angle), np.cos(angle)], axis=1)
    rows = np.stack([part.reshape(time_devs, -1, 2 * INNER) for part in (real_rows, imag_rows)], axis=1)
    rows = rows.reshape(4, 2, 4, -1).transpose(1, 0, 2, 3)
    return rows.reshape(INNER, 2 * INNER).astype(ml_dtypes.bfloat16)


def real_transform8(f):
    root = math.sqrt(0.5)
    a = [f[n] + f[n + 4] for n in range(4)]
    b = [f[n] - f[n + 4] for n in range(4)]
    low, high = root * (b[1] - b[3]), root * (b[1] + b[3])
    even, odd = a[0] + a[2], a[1] + a[3]
    return [
        (even + odd, None),
        (b[0] + low, -b[2] - high),
        (a[0] - a[2], a[3] - a[1]),
        (b[0] - low, b[2] - high),
        (even - odd, None),
    ]


def real_transform16(f):
    e = real_transform8(f[0::2])
    o = real_transform8(f[1::2])
    y = [None] * 9
    y[0] = (e[0][0] + o[0][0], None)
    y[8] = (e[0][0] - o[0][0], None)
    y[4] = (e[4][0], -o[4][0])
    for k in range(1, 4):
        cos, sin = math.cos(math.pi * k / 8), math.sin(math.pi * k / 8)
        re = o[k][0] * cos + o[k][1] * sin
        im = o[k][1] * cos - o[k][0] * sin
        y[k] = (e[k][0] + re, e[k][1] + im)
        y[8 - k] = (e[k][0] - re, im - e[k][1])
    return y


def spectra_kernel(spectra_taps, outs, volts_ref, window_ref, twiddle_ref, table_ref, side_ref, *refs):
    out_refs, z_ref = refs[:-1], refs[-1]
    paths = volts_ref.shape[0]
    strip = 16

    def block(lane, carry):
        for s, taps in enumerate(spectra_taps):
            for top in range(0, paths, strip):
                f = []
                for n1 in range(RADIX):
                    total = None
                    for tap, number in taps:
                        start = number * FFT_LEN + n1 * INNER
                        at = pl.ds(pl.multiple_of(start + lane * LANES, LANES), LANES)
                        w_at = pl.ds(pl.multiple_of(n1 * INNER + lane * LANES, LANES), LANES)
                        volts = volts_ref[top : top + strip, at].astype(jnp.float32)
                        term = window_ref[tap : tap + 1, w_at] * volts
                        total = term if total is None else total + term
                    f.append(total.astype(jnp.bfloat16).astype(jnp.float32))
                y = real_transform16(f)
                re_at = pl.ds(pl.multiple_of(lane * LANES, LANES), LANES)
                im_at = pl.ds(pl.multiple_of(INNER + lane * LANES, LANES), LANES)
                for k1 in range(RADIX):
                    re, im = y[min(k1, RADIX - k1)]
                    if k1 > RADIX - k1:
                        im = -im
                    if k1 == 0:
                        z_re, z_im = re, jnp.zeros_like(re)
                    else:
                        cos = twiddle_ref[k1 : k1 + 1, re_at]
                        sin = twiddle_ref[RADIX + k1 : RADIX + k1 + 1, re_at]
                        if im is None:
                            z_re, z_im = re * cos, -re * sin
                        else:
                            z_re, z_im = re * cos + im * sin, im * cos - re * sin
                    row = ((s // HALF * (RADIX // 4) + k1 // 4) * HALF + s % HALF) * 4 * paths
                    row += (k1 % 4) * paths + top
                    z_ref[row : row + strip, re_at] = z_re.astype(jnp.bfloat16)
                    z_ref[row : row + strip, im_at] = z_im.astype(jnp.bfloat16)
        return carry

    lax.fori_loop(0, INNER // LANES, block, 0)

    rows = INNER // 2

    def product(number, carry):
        at = pl.ds(pl.multiple_of((number ^ side_ref[0]) * rows, rows), rows)
        result = lax.dot_general(
            table_ref[at, :], z_ref[...], NT, preferred_element_type=jnp.float32
        ).astype(jnp.bfloat16)

        for (part, start), ref in zip(outs, out_refs):
            @pl.when(number == part)
            def _():
                ref[...] = result[:, start : start + ref.shape[1]]

        return carry

    lax.fori_loop(0, 2, product, 0)


def spectra(volts, window, twiddle, table, side, spectra_taps, outs):
    paths = volts.shape[0]
    lanes = RADIX * len(spectra_taps) * paths
    out = [jax.ShapeDtypeStruct((INNER // 2, count), jnp.bfloat16) for _, _, count in outs]
    whole = lambda x: pl.BlockSpec(x.shape, lambda i: (0, 0))
    return pl.pallas_call(
        functools.partial(spectra_kernel, spectra_taps, [o[:2] for o in outs]),
        grid=(1,),
        out_shape=out,
        in_specs=[whole(x) for x in (volts, window, twiddle, table)] + [pl.BlockSpec(memory_space=pltpu.SMEM)],
        out_specs=[whole(x) for x in out],
        scratch_shapes=[pltpu.VMEM((lanes, 2 * INNER), jnp.bfloat16)],
        compiler_params=pltpu.CompilerParams(vmem_limit_bytes=VMEM_BYTES),
        cost_estimate=pl.CostEstimate(flops=2**20, bytes_accessed=20 * 2**20, transcendentals=0),
        name="spectra",
    )(volts, window, twiddle, table, side)


def gram_kernel(*refs):
    parts = [refs[4 * n : 4 * n + 4] for n in range(4)]
    carries = (None, None, parts[3], parts[2])
    place_ref, own_ref, mask_ref, rank_ref = refs[16:20]
    out_ref, g_ref, o_ref = refs[-3:]
    times, rows, width = parts[0][0].shape
    chans = rows // 2
    total = 4 * HALF * times
    groups = width // (HALF * LANES)

    @pl.when(pl.program_id(0) == 0)
    def _():
        def regroup(number, carry):
            s = lax.rem(number, HALF)
            low = number // HALF * 4
            lanes = pl.ds(pl.multiple_of(number * LANES, LANES), LANES)
            left = []
            for sources, extra in zip(parts, carries):
                pieces = []
                for e, ref in enumerate(sources):
                    piece = ref[:times, :, lanes]
                    if extra is not None:
                        piece = piece.reshape(times // 4, 4, rows, LANES)
                        first = piece[:, :1] + extra[e][times:, :, lanes].reshape(times // 4, 1, rows, LANES)
                        piece = jnp.concatenate([first, piece[:, 1:]], axis=1)
                    pieces.append(piece.reshape(times * rows, LANES))
                left.append(jnp.concatenate(pieces, axis=1))
            left = jnp.concatenate(left, axis=0)
            moved = jnp.dot(left, place_ref[...], preferred_element_type=jnp.float32)
            mine = left[:, :LANES].astype(jnp.float32)
            for n in range(len(parts)):
                for t in range(times):
                    rank = rank_ref[(n * HALF + s) * times + t]
                    at = pl.ds(pl.multiple_of(rank * rows, rows), rows)
                    here = slice((n * times + t) * rows, (n * times + t + 1) * rows)
                    o_ref[number // HALF, at, :] = mine[here]
                    for l in range(4):
                        g_ref[low + l, at, :] = moved[here, l * LANES : (l + 1) * LANES]
            return carry

        lax.fori_loop(0, groups * HALF, regroup, 0)

    chan = pl.program_id(0)
    side = total // 2
    paths = LANES // 4
    shape = (NBINS // 2, paths, LANES)

    def scaled(ref, low):
        re = ref[low, pl.ds(chan, total, stride=rows), :]
        im = ref[low, pl.ds(chans + chan, total, stride=rows), :]
        power = jnp.sum(re * re + im * im, axis=0, keepdims=True)
        equalizer = lax.rsqrt(power / total + 1e-06) * math.sqrt(NBINS / total)
        return (re * equalizer).astype(jnp.bfloat16), (im * equalizer).astype(jnp.bfloat16)

    halves = [slice(half * side, (half + 1) * side) for half in range(2)]
    for group in range(groups):
        re, im = scaled(o_ref, group)
        turned_own = [
            lax.dot_general(
                own_ref[...], jnp.concatenate([re[at], im[at]], axis=0), NT, preferred_element_type=jnp.float32
            ).astype(jnp.bfloat16)
            for at in halves
        ]
        for l in range(4):
            low = group * 4 + l
            re, im = scaled(g_ref, low)
            for half, at in enumerate(halves):
                left = turned_own[half][l * paths : (l + 1) * paths]
                left = jnp.concatenate([left] * (NBINS // 2), axis=0) * mask_ref[...]
                both = jnp.concatenate([re[at], im[at]], axis=0)
                turned = jnp.concatenate([-im[at], re[at]], axis=0)
                right = jnp.concatenate([both, turned], axis=1)
                result = jnp.dot(left, right, preferred_element_type=jnp.float32).astype(jnp.bfloat16)
                bins = slice(half * NBINS // 2, (half + 1) * NBINS // 2)
                out_ref[0, low, bins, 0] = result[:, :LANES].reshape(shape)
                out_ref[0, low, bins, 1] = result[:, LANES:].reshape(shape)


def grams(sources, place, own, mask, rank, part, before):
    times, rows, _ = sources[0].shape
    chans = rows // 2
    paths = own.shape[0] // 4
    lanes = RADIX // 2 * HALF * paths
    lows = RADIX // 2

    def block(x):
        at = part if x.shape[2] > lanes else 0
        return pl.BlockSpec((x.shape[0], rows, lanes), lambda j: (0, 0, at))

    args = (*sources, place, own, mask, rank)
    in_specs = [block(x) for x in sources] + [
        pl.BlockSpec(place.shape, lambda j: (0, 0)),
        pl.BlockSpec(own.shape, lambda j: (0, 0)),
        pl.BlockSpec(mask.shape, lambda j: (0, 0)),
        pl.BlockSpec(memory_space=pltpu.SMEM),
    ]
    aliases = {}
    if before is not None:
        aliases = {len(args): 0}
        args += (before,)
        in_specs.append(pl.BlockSpec(memory_space=pl.ANY))
    return pl.pallas_call(
        gram_kernel,
        grid=(chans,),
        out_shape=jax.ShapeDtypeStruct((chans, RADIX, NBINS, 2, paths, LANES), jnp.bfloat16),
        in_specs=in_specs,
        out_specs=pl.BlockSpec((1, lows, NBINS, 2, paths, LANES), lambda j: (j, part, 0, 0, 0, 0)),
        scratch_shapes=[
            pltpu.VMEM((lows, rank.shape[0] * rows, LANES), jnp.float32),
            pltpu.VMEM((lows // 4, rank.shape[0] * rows, LANES), jnp.float32),
        ],
        input_output_aliases=aliases,
        compiler_params=pltpu.CompilerParams(vmem_limit_bytes=VMEM_BYTES),
        cost_estimate=pl.CostEstimate(flops=9 * 2**29, bytes_accessed=15 * 2**20, transcendentals=0),
        name="grams",
    )(*args)


def join_kernel(parts, pins, x_ref, side_ref, *refs):
    out_refs = refs[pins:]
    width = x_ref.shape[2] // 2
    for (first, count), out_ref in zip(parts, out_refs):
        own = slice(first, first + count)
        carry = slice(width + first, width + first + count)
        for t in range(16):
            value = x_ref[t, :, own]
            if t % 4:
                value = value.astype(jnp.float32) + x_ref[t - 1, :, carry].astype(jnp.float32)
            out_ref[t] = value.astype(jnp.bfloat16)

        @pl.when(side_ref[0] == 0)
        def _():
            for y in range(4):
                out_ref[16 + y] = x_ref[4 * y + 3, :, carry]

        @pl.when(side_ref[0] != 0)
        def _():
            out_ref[16] = jnp.zeros(out_ref.shape[1:], out_ref.dtype)
            for y in range(3):
                out_ref[17 + y] = x_ref[4 * y + 3, :, carry]


def joined(x, z_hi, parts, *others):
    outs = [jax.ShapeDtypeStruct((20, x.shape[1], count), x.dtype) for _, count in parts]
    return pl.pallas_call(
        functools.partial(join_kernel, parts, len(others)),
        grid=(1,),
        out_shape=outs,
        in_specs=[pl.BlockSpec(x.shape, lambda i: (0, 0, 0)), pl.BlockSpec(memory_space=pltpu.SMEM)]
        + [pl.BlockSpec(memory_space=pltpu.HBM)] * len(others),
        out_specs=[pl.BlockSpec(o.shape, lambda i: (0, 0, 0)) for o in outs],
        cost_estimate=pl.CostEstimate(flops=2**20, bytes_accessed=2**20, transcendentals=0),
        compiler_params=pltpu.CompilerParams(vmem_limit_bytes=16 * 1024 * 1024),
        name="joined",
    )(x, z_hi, *others)


def follows(x, *others):
    return pl.pallas_call(
        lambda *refs: None,
        out_shape=jax.ShapeDtypeStruct(x.shape, x.dtype),
        in_specs=[pl.BlockSpec(memory_space=pltpu.HBM)] * (1 + len(others)),
        out_specs=pl.BlockSpec(memory_space=pltpu.HBM),
        input_output_aliases={0: 0},
        cost_estimate=pl.CostEstimate(flops=0, bytes_accessed=0, transcendentals=0),
        name="follows",
    )(x, *others)


def swapped(x, by):
    return lax.ppermute(x, "pol", [(i, i ^ by) for i in range(4)])


def on_device(voltages, phase_bin):
    paths = voltages.shape[0]
    time_devs = lax.axis_size("tm")
    path_devs = lax.axis_size("pol")
    total = time_devs * 2 * HALF
    window = jnp.asarray(filter_window())
    twiddle = jnp.asarray(twiddles())
    table = jnp.asarray(inner_table(time_devs))

    me = lax.axis_index("pol")
    src = jnp.arange(4 * LANES, dtype=jnp.int32)[:, None]
    dst = jnp.arange(4 * LANES, dtype=jnp.int32)[None, :]
    device = jnp.bitwise_xor(src // LANES, me)
    target = (src % LANES) // paths * LANES + device * paths + src % paths
    place = (target == dst).astype(jnp.bfloat16)
    own = jnp.eye(LANES, dtype=jnp.bfloat16)
    t_at = lax.axis_index("tm")
    side = t_at // 4 % 2
    order = np.arange(total).reshape(4, 2, 4, 2, HALF)[:, :, :, ::-1].transpose(3, 1, 4, 0, 2)
    order = np.stack([order, order[:, ::-1]]).reshape(2, total)
    pick = (order[:, :, None] == np.arange(total)).astype(np.float32)
    pick = jnp.where(side == 0, jnp.asarray(pick[0]), jnp.asarray(pick[1]))
    labels = jnp.sum(pick * phase_bin.astype(jnp.float32)[None, :], axis=1).astype(jnp.int32)
    number = jnp.arange(total, dtype=jnp.int32)
    ahead = (labels[:, None] == labels[None, :]) & (number[:, None] > number[None, :])
    rank = labels * (total // NBINS) + jnp.sum(ahead.astype(jnp.int32), axis=1)
    rank = jnp.clip(rank, 0, total - 1)
    mask = np.arange(NBINS // 2)[:, None] == np.arange(total // 2)[None, :] // (total // NBINS)
    mask = jnp.asarray(np.repeat(np.tile(mask, (1, 2)), paths, axis=0).astype(ml_dtypes.bfloat16))

    groups = [[y * 8 + z * 4 + x for y in range(4) for x in range(4)] for z in range(2)]
    across = []
    for t in range(time_devs):
        for q in range(path_devs):
            across.append((t * path_devs + q, (t ^ 4) * path_devs + (q ^ 2)))

    def exchanged(x):
        x = x.reshape(time_devs // 2, INNER // time_devs, -1)
        return lax.all_to_all(
            x, "tm", split_axis=0, concat_axis=0, axis_index_groups=groups, tiled=True
        )

    def crossed(x):
        return lax.ppermute(x, ("tm", "pol"), across)

    def after(x, *others):
        return lax.optimization_barrier((x, *others))[0]

    def own_set(x, z):
        return (x, swapped(x, 1), z, swapped(z, 1))

    def cross_set(x, z):
        return (z, swapped(z, 1), x, swapped(x, 1))

    side = side.reshape(1).astype(jnp.int32)
    full = [[(tap, s + tap) for tap in range(TAPS)] for s in range(HALF)]
    part = [[(tap, s + tap - HALF) for tap in range(TAPS) if s + tap >= HALF] for s in range(HALF)]
    carry = [[(tap, s + tap + HALF) for tap in range(TAPS) if s + tap < HALF] for s in range(HALF)]

    wide = RADIX * HALF * paths
    late, late_x = spectra(voltages, window, twiddle, table, side, full, [(0, 0, wide), (1, 0, wide)])
    early_side = side + jnp.minimum(rank[:1], 0)
    early, part_x, carry_x = spectra(
        voltages, window, twiddle, table, early_side, part + carry,
        [(0, 0, 2 * wide), (1, 0, wide), (1, wide, wide)],
    )
    late_x = crossed(late_x)
    part_x = crossed(part_x)
    carry_x = crossed(carry_x)
    late = exchanged(late)
    late_z = swapped(late, 2)
    late_c = swapped(late, 1)
    late_x = exchanged(follows(late_x, late, early))
    late_xz = swapped(late_x, 2)
    late_xc = swapped(late_x, 1)
    late_zc = swapped(late_z, 1)
    early = exchanged(follows(early, late_x, late_z, part_x))
    early_x = exchanged(follows(jnp.concatenate([part_x, carry_x], axis=1), early))
    (early,) = joined(early, side, [(0, wide)], late_xz)
    early_z = swapped(early, 2)
    low, high = joined(early_x, 1 - side, [(0, wide // 2), (wide // 2, wide // 2)])
    low_z = swapped(low, 2)
    low_c = swapped(low, 1)
    high_c = swapped(high, 1)
    late_xzc = swapped(late_xz, 1)
    early_c = swapped(early, 1)
    early_zc = swapped(early_z, 1)
    common = (late, late_c, late_z, late_zc, late_xz, late_xzc, late_x, late_xc)
    common += (early, early_c, early_z, early_zc)
    high = follows(high, low_z, late_c, late_zc, late_xzc, late_xc, early_c, early_zc, low_c)
    high_z = swapped(high, 2)
    out = grams(common + (low_z, swapped(low_z, 1), low, low_c), place, own, mask, rank, 0, None)
    high_z = follows(high_z, out)
    out = grams(common + (high_z, swapped(high_z, 1), high, high_c), place, own, mask, rank, 1, out)
    return out.reshape(CHANNELS // time_devs, NBINS, 2, paths, paths * path_devs)


def solution(mesh):
    in_specs = (P("pol", "tm"), P())
    out_specs = P("tm", None, None, "pol", None)
    return jax.shard_map(
        on_device, mesh=mesh, in_specs=in_specs, out_specs=out_specs, check_vma=False
    )
```

```python
import functools
import math

import jax
import jax.numpy as jnp
import ml_dtypes
import numpy as np
from jax import lax
from jax.experimental import pallas as pl
from jax.experimental.pallas import tpu as pltpu
from jax.sharding import PartitionSpec as P

FFT_LEN = 8192
TAPS = 4
NBINS = 8
CHANNELS = 4096
RADIX = 16
INNER = FFT_LEN // RADIX
LANES = 128
PITCH = 24
VMEM_BYTES = 63 * 1024 * 1024
HALF = 3
NT = (((1,), (1,)), ((), ()))


def filter_window():
    length = TAPS * FFT_LEN
    place = np.arange(length, dtype=np.float64)
    center = (place - length / 2 + 0.5) / FFT_LEN
    taper = 0.5 - 0.5 * np.cos(2.0 * math.pi * (place + 0.5) / length)
    return (np.sinc(center) * taper).reshape(TAPS, FFT_LEN).astype(np.float32)


def twiddles():
    angle = 2.0 * math.pi * np.outer(np.arange(RADIX), np.arange(INNER)) / FFT_LEN
    return np.concatenate([np.cos(angle), np.sin(angle)]).astype(np.float32)


def inner_table(time_devs):
    angle = 2.0 * math.pi * (np.outer(np.arange(INNER // 2), np.arange(INNER)) % INNER) / INNER
    real_rows = np.concatenate([np.cos(angle), np.sin(angle)], axis=1)
    imag_rows = np.concatenate([-np.sin(angle), np.cos(angle)], axis=1)
    rows = np.stack([part.reshape(time_devs, -1, 2 * INNER) for part in (real_rows, imag_rows)], axis=1)
    rows = rows.reshape(4, 2, 4, -1).transpose(1, 0, 2, 3)
    return rows.reshape(INNER, 2 * INNER).astype(ml_dtypes.bfloat16)


def real_transform8(f):
    root = math.sqrt(0.5)
    a = [f[n] + f[n + 4] for n in range(4)]
    b = [f[n] - f[n + 4] for n in range(4)]
    low, high = root * (b[1] - b[3]), root * (b[1] + b[3])
    even, odd = a[0] + a[2], a[1] + a[3]
    return [
        (even + odd, None),
        (b[0] + low, -b[2] - high),
        (a[0] - a[2], a[3] - a[1]),
        (b[0] - low, b[2] - high),
        (even - odd, None),
    ]


def real_transform16(f):
    e = real_transform8(f[0::2])
    o = real_transform8(f[1::2])
    y = [None] * 9
    y[0] = (e[0][0] + o[0][0], None)
    y[8] = (e[0][0] - o[0][0], None)
    y[4] = (e[4][0], -o[4][0])
    for k in range(1, 4):
        cos, sin = math.cos(math.pi * k / 8), math.sin(math.pi * k / 8)
        re = o[k][0] * cos + o[k][1] * sin
        im = o[k][1] * cos - o[k][0] * sin
        y[k] = (e[k][0] + re, e[k][1] + im)
        y[8 - k] = (e[k][0] - re, im - e[k][1])
    return y


def spectra_kernel(spectra_taps, outs, volts_ref, window_ref, twiddle_ref, table_ref, side_ref, *refs):
    out_refs, z_ref = refs[:-1], refs[-1]
    paths = volts_ref.shape[0]
    strip = 16

    def block(lane, carry):
        for s, taps in enumerate(spectra_taps):
            for top in range(0, paths, strip):
                f = []
                for n1 in range(RADIX):
                    total = None
                    for tap, number in taps:
                        start = number * FFT_LEN + n1 * INNER
                        at = pl.ds(pl.multiple_of(start + lane * LANES, LANES), LANES)
                        w_at = pl.ds(pl.multiple_of(n1 * INNER + lane * LANES, LANES), LANES)
                        volts = volts_ref[top : top + strip, at].astype(jnp.float32)
                        term = window_ref[tap : tap + 1, w_at] * volts
                        total = term if total is None else total + term
                    f.append(total.astype(jnp.bfloat16).astype(jnp.float32))
                y = real_transform16(f)
                re_at = pl.ds(pl.multiple_of(lane * LANES, LANES), LANES)
                im_at = pl.ds(pl.multiple_of(INNER + lane * LANES, LANES), LANES)
                for k1 in range(RADIX):
                    re, im = y[min(k1, RADIX - k1)]
                    if k1 > RADIX - k1:
                        im = -im
                    if k1 == 0:
                        z_re, z_im = re, jnp.zeros_like(re)
                    else:
                        cos = twiddle_ref[k1 : k1 + 1, re_at]
                        sin = twiddle_ref[RADIX + k1 : RADIX + k1 + 1, re_at]
                        if im is None:
                            z_re, z_im = re * cos, -re * sin
                        else:
                            z_re, z_im = re * cos + im * sin, im * cos - re * sin
                    row = ((s // HALF * (RADIX // 4) + k1 // 4) * HALF + s % HALF) * 4 * paths
                    row += (k1 % 4) * paths + top
                    z_ref[row : row + strip, re_at] = z_re.astype(jnp.bfloat16)
                    z_ref[row : row + strip, im_at] = z_im.astype(jnp.bfloat16)
        return carry

    lax.fori_loop(0, INNER // LANES, block, 0)

    rows = INNER // 2

    def product(number, carry):
        at = pl.ds(pl.multiple_of((number ^ side_ref[0]) * rows, rows), rows)
        result = lax.dot_general(
            table_ref[at, :], z_ref[...], NT, preferred_element_type=jnp.float32
        ).astype(jnp.bfloat16)

        for (part, start), ref in zip(outs, out_refs):
            @pl.when(number == part)
            def _():
                ref[...] = result[:, start : start + ref.shape[1]]

        return carry

    lax.fori_loop(0, 2, product, 0)


def spectra(volts, window, twiddle, table, side, spectra_taps, outs):
    paths = volts.shape[0]
    lanes = RADIX * len(spectra_taps) * paths
    out = [jax.ShapeDtypeStruct((INNER // 2, count), jnp.bfloat16) for _, _, count in outs]
    whole = lambda x: pl.BlockSpec(x.shape, lambda i: (0, 0))
    return pl.pallas_call(
        functools.partial(spectra_kernel, spectra_taps, [o[:2] for o in outs]),
        grid=(1,),
        out_shape=out,
        in_specs=[whole(x) for x in (volts, window, twiddle, table)] + [pl.BlockSpec(memory_space=pltpu.SMEM)],
        out_specs=[whole(x) for x in out],
        scratch_shapes=[pltpu.VMEM((lanes, 2 * INNER), jnp.bfloat16)],
        compiler_params=pltpu.CompilerParams(vmem_limit_bytes=VMEM_BYTES),
        cost_estimate=pl.CostEstimate(flops=2**20, bytes_accessed=20 * 2**20, transcendentals=0),
        name="spectra",
    )(volts, window, twiddle, table, side)


def gram_kernel(*refs):
    parts = [refs[4 * n : 4 * n + 4] for n in range(4)]
    carries = (None, None, parts[3], parts[2])
    place_ref, own_ref, mask_ref, rank_ref = refs[16:20]
    out_ref, g_ref, o_ref = refs[-3:]
    times, rows, width = parts[0][0].shape
    chans = rows // 2
    total = 4 * HALF * times
    groups = width // (HALF * LANES)

    @pl.when(pl.program_id(0) == 0)
    def _():
        def regroup(number, carry):
            s = lax.rem(number, HALF)
            low = number // HALF * 4
            lanes = pl.ds(pl.multiple_of(number * LANES, LANES), LANES)
            left = []
            for sources, extra in zip(parts, carries):
                pieces = []
                for e, ref in enumerate(sources):
                    piece = ref[:times, :, lanes]
                    if extra is not None:
                        piece = piece.reshape(times // 4, 4, rows, LANES)
                        first = piece[:, :1] + extra[e][times:, :, lanes].reshape(times // 4, 1, rows, LANES)
                        piece = jnp.concatenate([first, piece[:, 1:]], axis=1)
                    pieces.append(piece.reshape(times * rows, LANES))
                left.append(jnp.concatenate(pieces, axis=1))
            left = jnp.concatenate(left, axis=0)
            moved = jnp.dot(left, place_ref[...], preferred_element_type=jnp.float32)
            mine = left[:, :LANES].astype(jnp.float32)
            for n in range(len(parts)):
                for t in range(times):
                    rank = rank_ref[(n * HALF + s) * times + t]
                    at = pl.ds(pl.multiple_of(rank * PITCH, 8), rows)
                    here = slice((n * times + t) * rows, (n * times + t + 1) * rows)
                    o_ref[number // HALF, at, :] = mine[here]
                    for l in range(4):
                        g_ref[low + l, at, :] = moved[here, l * LANES : (l + 1) * LANES]
            return carry

        lax.fori_loop(0, groups * HALF, regroup, 0)

    chan = pl.program_id(0)
    side = total // 2
    paths = LANES // 4
    shape = (NBINS // 2, paths, LANES)

    def scaled(ref, low):
        re = ref[low, pl.ds(chan, total, stride=PITCH), :]
        im = ref[low, pl.ds(chans + chan, total, stride=PITCH), :]
        power = jnp.sum(re * re + im * im, axis=0, keepdims=True)
        equalizer = lax.rsqrt(power / total + 1e-06) * math.sqrt(NBINS / total)
        return (re * equalizer).astype(jnp.bfloat16), (im * equalizer).astype(jnp.bfloat16)

    halves = [slice(half * side, (half + 1) * side) for half in range(2)]
    for group in range(groups):
        re, im = scaled(o_ref, group)
        turned_own = [
            lax.dot_general(
                own_ref[...], jnp.concatenate([re[at], im[at]], axis=0), NT, preferred_element_type=jnp.float32
            ).astype(jnp.bfloat16)
            for at in halves
        ]
        for l in range(4):
            low = group * 4 + l
            re, im = scaled(g_ref, low)
            for half, at in enumerate(halves):
                left = turned_own[half][l * paths : (l + 1) * paths]
                left = jnp.concatenate([left] * (NBINS // 2), axis=0) * mask_ref[...]
                both = jnp.concatenate([re[at], im[at]], axis=0)
                turned = jnp.concatenate([-im[at], re[at]], axis=0)
                right = jnp.concatenate([both, turned], axis=1)
                result = jnp.dot(left, right, preferred_element_type=jnp.float32).astype(jnp.bfloat16)
                bins = slice(half * NBINS // 2, (half + 1) * NBINS // 2)
                out_ref[0, low, bins, 0] = result[:, :LANES].reshape(shape)
                out_ref[0, low, bins, 1] = result[:, LANES:].reshape(shape)


def grams(sources, place, own, mask, rank, part, before):
    times, rows, _ = sources[0].shape
    chans = rows // 2
    paths = own.shape[0] // 4
    lanes = RADIX // 2 * HALF * paths
    lows = RADIX // 2

    def block(x):
        at = part if x.shape[2] > lanes else 0
        return pl.BlockSpec((x.shape[0], rows, lanes), lambda j: (0, 0, at))

    args = (*sources, place, own, mask, rank)
    in_specs = [block(x) for x in sources] + [
        pl.BlockSpec(place.shape, lambda j: (0, 0)),
        pl.BlockSpec(own.shape, lambda j: (0, 0)),
        pl.BlockSpec(mask.shape, lambda j: (0, 0)),
        pl.BlockSpec(memory_space=pltpu.SMEM),
    ]
    aliases = {}
    if before is not None:
        aliases = {len(args): 0}
        args += (before,)
        in_specs.append(pl.BlockSpec(memory_space=pl.ANY))
    return pl.pallas_call(
        gram_kernel,
        grid=(chans,),
        out_shape=jax.ShapeDtypeStruct((chans, RADIX, NBINS, 2, paths, LANES), jnp.bfloat16),
        in_specs=in_specs,
        out_specs=pl.BlockSpec((1, lows, NBINS, 2, paths, LANES), lambda j: (j, part, 0, 0, 0, 0)),
        scratch_shapes=[
            pltpu.VMEM((lows, rank.shape[0] * PITCH, LANES), jnp.float32),
            pltpu.VMEM((lows // 4, rank.shape[0] * PITCH, LANES), jnp.float32),
        ],
        input_output_aliases=aliases,
        compiler_params=pltpu.CompilerParams(vmem_limit_bytes=VMEM_BYTES),
        cost_estimate=pl.CostEstimate(flops=9 * 2**29, bytes_accessed=15 * 2**20, transcendentals=0),
        name="grams",
    )(*args)


def join_kernel(parts, pins, x_ref, side_ref, *refs):
    out_refs = refs[pins:]
    width = x_ref.shape[2] // 2
    for (first, count), out_ref in zip(parts, out_refs):
        own = slice(first, first + count)
        carry = slice(width + first, width + first + count)
        for t in range(16):
            value = x_ref[t, :, own]
            if t % 4:
                value = value.astype(jnp.float32) + x_ref[t - 1, :, carry].astype(jnp.float32)
            out_ref[t] = value.astype(jnp.bfloat16)

        @pl.when(side_ref[0] == 0)
        def _():
            for y in range(4):
                out_ref[16 + y] = x_ref[4 * y + 3, :, carry]

        @pl.when(side_ref[0] != 0)
        def _():
            out_ref[16] = jnp.zeros(out_ref.shape[1:], out_ref.dtype)
            for y in range(3):
                out_ref[17 + y] = x_ref[4 * y + 3, :, carry]


def joined(x, z_hi, parts, *others):
    outs = [jax.ShapeDtypeStruct((20, x.shape[1], count), x.dtype) for _, count in parts]
    return pl.pallas_call(
        functools.partial(join_kernel, parts, len(others)),
        grid=(1,),
        out_shape=outs,
        in_specs=[pl.BlockSpec(x.shape, lambda i: (0, 0, 0)), pl.BlockSpec(memory_space=pltpu.SMEM)]
        + [pl.BlockSpec(memory_space=pltpu.HBM)] * len(others),
        out_specs=[pl.BlockSpec(o.shape, lambda i: (0, 0, 0)) for o in outs],
        cost_estimate=pl.CostEstimate(flops=2**20, bytes_accessed=2**20, transcendentals=0),
        compiler_params=pltpu.CompilerParams(vmem_limit_bytes=16 * 1024 * 1024),
        name="joined",
    )(x, z_hi, *others)


def follows(x, *others):
    return pl.pallas_call(
        lambda *refs: None,
        out_shape=jax.ShapeDtypeStruct(x.shape, x.dtype),
        in_specs=[pl.BlockSpec(memory_space=pltpu.HBM)] * (1 + len(others)),
        out_specs=pl.BlockSpec(memory_space=pltpu.HBM),
        input_output_aliases={0: 0},
        cost_estimate=pl.CostEstimate(flops=0, bytes_accessed=0, transcendentals=0),
        name="follows",
    )(x, *others)


def swapped(x, by):
    return lax.ppermute(x, "pol", [(i, i ^ by) for i in range(4)])


def on_device(voltages, phase_bin):
    paths = voltages.shape[0]
    time_devs = lax.axis_size("tm")
    path_devs = lax.axis_size("pol")
    total = time_devs * 2 * HALF
    window = jnp.asarray(filter_window())
    twiddle = jnp.asarray(twiddles())
    table = jnp.asarray(inner_table(time_devs))

    me = lax.axis_index("pol")
    src = jnp.arange(4 * LANES, dtype=jnp.int32)[:, None]
    dst = jnp.arange(4 * LANES, dtype=jnp.int32)[None, :]
    device = jnp.bitwise_xor(src // LANES, me)
    target = (src % LANES) // paths * LANES + device * paths + src % paths
    place = (target == dst).astype(jnp.bfloat16)
    own = jnp.asarray(np.eye(LANES).astype(ml_dtypes.bfloat16))
    t_at = lax.axis_index("tm")
    side = t_at // 4 % 2
    order = np.arange(total).reshape(4, 2, 4, 2, HALF)[:, :, :, ::-1].transpose(3, 1, 4, 0, 2)
    order = np.stack([order, order[:, ::-1]]).reshape(2, total)
    pick = (order[:, :, None] == np.arange(total)).astype(np.float32)
    pick = jnp.where(side == 0, jnp.asarray(pick[0]), jnp.asarray(pick[1]))
    labels = jnp.sum(pick * phase_bin.astype(jnp.float32)[None, :], axis=1).astype(jnp.int32)
    number = jnp.arange(total, dtype=jnp.int32)
    ahead = (labels[:, None] == labels[None, :]) & (number[:, None] > number[None, :])
    rank = labels * (total // NBINS) + jnp.sum(ahead.astype(jnp.int32), axis=1)
    rank = jnp.clip(rank, 0, total - 1)
    mask = np.arange(NBINS // 2)[:, None] == np.arange(total // 2)[None, :] // (total // NBINS)
    mask = jnp.asarray(np.repeat(np.tile(mask, (1, 2)), paths, axis=0).astype(ml_dtypes.bfloat16))

    groups = [[y * 8 + z * 4 + x for y in range(4) for x in range(4)] for z in range(2)]
    across = []
    for t in range(time_devs):
        for q in range(path_devs):
            across.append((t * path_devs + q, (t ^ 4) * path_devs + (q ^ 2)))

    def exchanged(x):
        x = x.reshape(time_devs // 2, INNER // time_devs, -1)
        return lax.all_to_all(
            x, "tm", split_axis=0, concat_axis=0, axis_index_groups=groups, tiled=True
        )

    def crossed(x):
        return lax.ppermute(x, ("tm", "pol"), across)

    def after(x, *others):
        return lax.optimization_barrier((x, *others))[0]

    def own_set(x, z):
        return (x, swapped(x, 1), z, swapped(z, 1))

    def cross_set(x, z):
        return (z, swapped(z, 1), x, swapped(x, 1))

    side = side.reshape(1).astype(jnp.int32)
    full = [[(tap, s + tap) for tap in range(TAPS)] for s in range(HALF)]
    part = [[(tap, s + tap - HALF) for tap in range(TAPS) if s + tap >= HALF] for s in range(HALF)]
    carry = [[(tap, s + tap + HALF) for tap in range(TAPS) if s + tap < HALF] for s in range(HALF)]

    wide = RADIX * HALF * paths
    late, late_x = spectra(voltages, window, twiddle, table, side, full, [(0, 0, wide), (1, 0, wide)])
    early, part_x, carry_x = spectra(
        voltages, window, twiddle, table, side, part + carry,
        [(0, 0, 2 * wide), (1, 0, wide), (1, wide, wide)],
    )
    late_x = crossed(late_x)
    part_x = crossed(part_x)
    carry_x = crossed(carry_x)
    late = exchanged(late)
    late_z = swapped(late, 2)
    late_c = swapped(late, 1)
    late_x = exchanged(follows(late_x, late, early))
    late_xz = swapped(late_x, 2)
    late_xc = swapped(late_x, 1)
    late_zc = swapped(late_z, 1)
    early = exchanged(follows(early, late_x, late_z, part_x))
    early_x = exchanged(follows(jnp.concatenate([part_x, carry_x], axis=1), early))
    (early,) = joined(early, side, [(0, wide)], late_xz, place, rank)
    early_z = swapped(early, 2)
    low, high = joined(early_x, 1 - side, [(0, wide // 2), (wide // 2, wide // 2)])
    low_z = swapped(low, 2)
    low_c = swapped(low, 1)
    high_c = swapped(high, 1)
    late_xzc = swapped(late_xz, 1)
    early_c = swapped(early, 1)
    early_zc = swapped(early_z, 1)
    common = (late, late_c, late_z, late_zc, late_xz, late_xzc, late_x, late_xc)
    common += (early, early_c, early_z, early_zc)
    high = follows(high, low_z, late_c, late_zc, late_xzc, late_xc, early_c, early_zc, low_c)
    high_z = swapped(high, 2)
    out = grams(common + (low_z, swapped(low_z, 1), low, low_c), place, own, mask, rank, 0, None)
    high_z = follows(high_z, out)
    out = grams(common + (high_z, swapped(high_z, 1), high, high_c), place, own, mask, rank, 1, out)
    return out.reshape(CHANNELS // time_devs, NBINS, 2, paths, paths * path_devs)


def solution(mesh):
    in_specs = (P("pol", "tm"), P())
    out_specs = P("tm", None, None, "pol", None)
    return jax.shard_map(
        on_device, mesh=mesh, in_specs=in_specs, out_specs=out_specs, check_vma=False
    )
```

```python
import functools
import math

import jax
import jax.numpy as jnp
import ml_dtypes
import numpy as np
from jax import lax
from jax.experimental import pallas as pl
from jax.experimental.pallas import tpu as pltpu
from jax.sharding import PartitionSpec as P

FFT_LEN = 8192
TAPS = 4
NBINS = 8
CHANNELS = 4096
RADIX = 16
INNER = FFT_LEN // RADIX
LANES = 128
PITCH = 24
VMEM_BYTES = 63 * 1024 * 1024
HALF = 3
NT = (((1,), (1,)), ((), ()))


def filter_window():
    length = TAPS * FFT_LEN
    place = np.arange(length, dtype=np.float64)
    center = (place - length / 2 + 0.5) / FFT_LEN
    taper = 0.5 - 0.5 * np.cos(2.0 * math.pi * (place + 0.5) / length)
    return (np.sinc(center) * taper).reshape(TAPS, FFT_LEN).astype(np.float32)


def twiddles():
    angle = 2.0 * math.pi * np.outer(np.arange(RADIX), np.arange(INNER)) / FFT_LEN
    return np.concatenate([np.cos(angle), np.sin(angle)]).astype(np.float32)


def inner_table(time_devs):
    angle = 2.0 * math.pi * (np.outer(np.arange(INNER // 2), np.arange(INNER)) % INNER) / INNER
    real_rows = np.concatenate([np.cos(angle), np.sin(angle)], axis=1)
    imag_rows = np.concatenate([-np.sin(angle), np.cos(angle)], axis=1)
    rows = np.stack([part.reshape(time_devs, -1, 2 * INNER) for part in (real_rows, imag_rows)], axis=1)
    rows = rows.reshape(4, 2, 4, -1).transpose(1, 0, 2, 3)
    return rows.reshape(INNER, 2 * INNER).astype(ml_dtypes.bfloat16)


def real_transform8(f):
    root = math.sqrt(0.5)
    a = [f[n] + f[n + 4] for n in range(4)]
    b = [f[n] - f[n + 4] for n in range(4)]
    low, high = root * (b[1] - b[3]), root * (b[1] + b[3])
    even, odd = a[0] + a[2], a[1] + a[3]
    return [
        (even + odd, None),
        (b[0] + low, -b[2] - high),
        (a[0] - a[2], a[3] - a[1]),
        (b[0] - low, b[2] - high),
        (even - odd, None),
    ]


def real_transform16(f):
    e = real_transform8(f[0::2])
    o = real_transform8(f[1::2])
    y = [None] * 9
    y[0] = (e[0][0] + o[0][0], None)
    y[8] = (e[0][0] - o[0][0], None)
    y[4] = (e[4][0], -o[4][0])
    for k in range(1, 4):
        cos, sin = math.cos(math.pi * k / 8), math.sin(math.pi * k / 8)
        re = o[k][0] * cos + o[k][1] * sin
        im = o[k][1] * cos - o[k][0] * sin
        y[k] = (e[k][0] + re, e[k][1] + im)
        y[8 - k] = (e[k][0] - re, im - e[k][1])
    return y


def spectra_kernel(spectra_taps, outs, volts_ref, window_ref, twiddle_ref, table_ref, side_ref, *refs):
    out_refs, z_ref = refs[:-1], refs[-1]
    paths = volts_ref.shape[0]
    strip = 16

    def block(lane, carry):
        for s, taps in enumerate(spectra_taps):
            for top in range(0, paths, strip):
                f = []
                for n1 in range(RADIX):
                    total = None
                    for tap, number in taps:
                        start = number * FFT_LEN + n1 * INNER
                        at = pl.ds(pl.multiple_of(start + lane * LANES, LANES), LANES)
                        w_at = pl.ds(pl.multiple_of(n1 * INNER + lane * LANES, LANES), LANES)
                        volts = volts_ref[top : top + strip, at].astype(jnp.float32)
                        term = window_ref[tap : tap + 1, w_at] * volts
                        total = term if total is None else total + term
                    f.append(total.astype(jnp.bfloat16).astype(jnp.float32))
                y = real_transform16(f)
                re_at = pl.ds(pl.multiple_of(lane * LANES, LANES), LANES)
                im_at = pl.ds(pl.multiple_of(INNER + lane * LANES, LANES), LANES)
                for k1 in range(RADIX):
                    re, im = y[min(k1, RADIX - k1)]
                    if k1 > RADIX - k1:
                        im = -im
                    if k1 == 0:
                        z_re, z_im = re, jnp.zeros_like(re)
                    else:
                        cos = twiddle_ref[k1 : k1 + 1, re_at]
                        sin = twiddle_ref[RADIX + k1 : RADIX + k1 + 1, re_at]
                        if im is None:
                            z_re, z_im = re * cos, -re * sin
                        else:
                            z_re, z_im = re * cos + im * sin, im * cos - re * sin
                    row = ((s // HALF * (RADIX // 4) + k1 // 4) * HALF + s % HALF) * 4 * paths
                    row += (k1 % 4) * paths + top
                    z_ref[row : row + strip, re_at] = z_re.astype(jnp.bfloat16)
                    z_ref[row : row + strip, im_at] = z_im.astype(jnp.bfloat16)
        return carry

    lax.fori_loop(0, INNER // LANES, block, 0)

    rows = INNER // 2

    def product(number, carry):
        at = pl.ds(pl.multiple_of((number ^ side_ref[0]) * rows, rows), rows)
        result = lax.dot_general(
            table_ref[at, :], z_ref[...], NT, preferred_element_type=jnp.float32
        ).astype(jnp.bfloat16)

        for (part, start), ref in zip(outs, out_refs):
            @pl.when(number == part)
            def _():
                ref[...] = result[:, start : start + ref.shape[1]]

        return carry

    lax.fori_loop(0, 2, product, 0)


def spectra(volts, window, twiddle, table, side, spectra_taps, outs):
    paths = volts.shape[0]
    lanes = RADIX * len(spectra_taps) * paths
    out = [jax.ShapeDtypeStruct((INNER // 2, count), jnp.bfloat16) for _, _, count in outs]
    whole = lambda x: pl.BlockSpec(x.shape, lambda i: (0, 0))
    return pl.pallas_call(
        functools.partial(spectra_kernel, spectra_taps, [o[:2] for o in outs]),
        grid=(1,),
        out_shape=out,
        in_specs=[whole(x) for x in (volts, window, twiddle, table)] + [pl.BlockSpec(memory_space=pltpu.SMEM)],
        out_specs=[whole(x) for x in out],
        scratch_shapes=[pltpu.VMEM((lanes, 2 * INNER), jnp.bfloat16)],
        compiler_params=pltpu.CompilerParams(vmem_limit_bytes=VMEM_BYTES),
        cost_estimate=pl.CostEstimate(flops=2**20, bytes_accessed=20 * 2**20, transcendentals=0),
        name="spectra",
    )(volts, window, twiddle, table, side)


def gram_kernel(*refs):
    parts = [refs[4 * n : 4 * n + 4] for n in range(4)]
    carries = (None, None, parts[3], parts[2])
    place_ref, own_ref, mask_ref, rank_ref = refs[16:20]
    out_ref, g_ref, o_ref = refs[-3:]
    times, rows, width = parts[0][0].shape
    chans = rows // 2
    total = 4 * HALF * times
    groups = width // (HALF * LANES)

    @pl.when(pl.program_id(0) == 0)
    def _():
        def regroup(number, carry):
            s = lax.rem(number, HALF)
            low = number // HALF * 4
            lanes = pl.ds(pl.multiple_of(number * LANES, LANES), LANES)
            left = []
            for sources, extra in zip(parts, carries):
                pieces = []
                for e, ref in enumerate(sources):
                    piece = ref[:times, :, lanes]
                    if extra is not None:
                        piece = piece.reshape(times // 4, 4, rows, LANES)
                        first = piece[:, :1] + extra[e][times:, :, lanes].reshape(times // 4, 1, rows, LANES)
                        piece = jnp.concatenate([first, piece[:, 1:]], axis=1)
                    pieces.append(piece.reshape(times * rows, LANES))
                left.append(jnp.concatenate(pieces, axis=1))
            left = jnp.concatenate(left, axis=0)
            moved = jnp.dot(left, place_ref[...], preferred_element_type=jnp.float32)
            mine = left[:, :LANES].astype(jnp.float32)
            for n in range(len(parts)):
                for t in range(times):
                    rank = rank_ref[(n * HALF + s) * times + t]
                    at = pl.ds(pl.multiple_of(rank * PITCH, 8), rows)
                    here = slice((n * times + t) * rows, (n * times + t + 1) * rows)
                    o_ref[number // HALF, at, :] = mine[here]
                    for l in range(4):
                        g_ref[low + l, at, :] = moved[here, l * LANES : (l + 1) * LANES]
            return carry

        lax.fori_loop(0, groups * HALF, regroup, 0)

    chan = pl.program_id(0)
    side = total // 2
    paths = LANES // 4
    shape = (NBINS // 2, paths, LANES)

    def scaled(ref, low):
        re = ref[low, pl.ds(chan, total, stride=PITCH), :]
        im = ref[low, pl.ds(chans + chan, total, stride=PITCH), :]
        power = jnp.sum(re * re + im * im, axis=0, keepdims=True)
        equalizer = lax.rsqrt(power / total + 1e-06) * math.sqrt(NBINS / total)
        return (re * equalizer).astype(jnp.bfloat16), (im * equalizer).astype(jnp.bfloat16)

    halves = [slice(half * side, (half + 1) * side) for half in range(2)]
    for group in range(groups):
        re, im = scaled(o_ref, group)
        turned_own = [
            lax.dot_general(
                own_ref[...], jnp.concatenate([re[at], im[at]], axis=0), NT, preferred_element_type=jnp.float32
            ).astype(jnp.bfloat16)
            for at in halves
        ]
        for l in range(4):
            low = group * 4 + l
            re, im = scaled(g_ref, low)
            for half, at in enumerate(halves):
                left = turned_own[half][l * paths : (l + 1) * paths]
                left = jnp.concatenate([left] * (NBINS // 2), axis=0) * mask_ref[...]
                both = jnp.concatenate([re[at], im[at]], axis=0)
                turned = jnp.concatenate([-im[at], re[at]], axis=0)
                right = jnp.concatenate([both, turned], axis=1)
                result = jnp.dot(left, right, preferred_element_type=jnp.float32).astype(jnp.bfloat16)
                bins = slice(half * NBINS // 2, (half + 1) * NBINS // 2)
                out_ref[0, low, bins, 0] = result[:, :LANES].reshape(shape)
                out_ref[0, low, bins, 1] = result[:, LANES:].reshape(shape)


def grams(sources, place, own, mask, rank, part, before):
    times, rows, _ = sources[0].shape
    chans = rows // 2
    paths = own.shape[0] // 4
    lanes = RADIX // 2 * HALF * paths
    lows = RADIX // 2

    def block(x):
        at = part if x.shape[2] > lanes else 0
        return pl.BlockSpec((x.shape[0], rows, lanes), lambda j: (0, 0, at))

    args = (*sources, place, own, mask, rank)
    in_specs = [block(x) for x in sources] + [
        pl.BlockSpec(place.shape, lambda j: (0, 0)),
        pl.BlockSpec(own.shape, lambda j: (0, 0)),
        pl.BlockSpec(mask.shape, lambda j: (0, 0)),
        pl.BlockSpec(memory_space=pltpu.SMEM),
    ]
    aliases = {}
    if before is not None:
        aliases = {len(args): 0}
        args += (before,)
        in_specs.append(pl.BlockSpec(memory_space=pl.ANY))
    return pl.pallas_call(
        gram_kernel,
        grid=(chans,),
        out_shape=jax.ShapeDtypeStruct((chans, RADIX, NBINS, 2, paths, LANES), jnp.bfloat16),
        in_specs=in_specs,
        out_specs=pl.BlockSpec((1, lows, NBINS, 2, paths, LANES), lambda j: (j, part, 0, 0, 0, 0)),
        scratch_shapes=[
            pltpu.VMEM((lows, rank.shape[0] * PITCH, LANES), jnp.float32),
            pltpu.VMEM((lows // 4, rank.shape[0] * PITCH, LANES), jnp.float32),
        ],
        input_output_aliases=aliases,
        compiler_params=pltpu.CompilerParams(vmem_limit_bytes=VMEM_BYTES),
        cost_estimate=pl.CostEstimate(flops=9 * 2**29, bytes_accessed=15 * 2**20, transcendentals=0),
        name="grams",
    )(*args)


def join_kernel(parts, pins, x_ref, side_ref, *refs):
    out_refs = refs[pins:]
    width = x_ref.shape[2] // 2
    for (first, count), out_ref in zip(parts, out_refs):
        own = slice(first, first + count)
        carry = slice(width + first, width + first + count)
        for t in range(16):
            value = x_ref[t, :, own]
            if t % 4:
                value = value.astype(jnp.float32) + x_ref[t - 1, :, carry].astype(jnp.float32)
            out_ref[t] = value.astype(jnp.bfloat16)

        @pl.when(side_ref[0] == 0)
        def _():
            for y in range(4):
                out_ref[16 + y] = x_ref[4 * y + 3, :, carry]

        @pl.when(side_ref[0] != 0)
        def _():
            out_ref[16] = jnp.zeros(out_ref.shape[1:], out_ref.dtype)
            for y in range(3):
                out_ref[17 + y] = x_ref[4 * y + 3, :, carry]


def joined(x, z_hi, parts, *others):
    outs = [jax.ShapeDtypeStruct((20, x.shape[1], count), x.dtype) for _, count in parts]
    return pl.pallas_call(
        functools.partial(join_kernel, parts, len(others)),
        grid=(1,),
        out_shape=outs,
        in_specs=[pl.BlockSpec(x.shape, lambda i: (0, 0, 0)), pl.BlockSpec(memory_space=pltpu.SMEM)]
        + [pl.BlockSpec(memory_space=pltpu.HBM)] * len(others),
        out_specs=[pl.BlockSpec(o.shape, lambda i: (0, 0, 0)) for o in outs],
        cost_estimate=pl.CostEstimate(flops=2**20, bytes_accessed=2**20, transcendentals=0),
        compiler_params=pltpu.CompilerParams(vmem_limit_bytes=16 * 1024 * 1024),
        name="joined",
    )(x, z_hi, *others)


def beside(x, y):
    width = x.shape[1]
    out = jax.ShapeDtypeStruct((x.shape[0], width + y.shape[1]), x.dtype)

    def kernel(x_ref, y_ref, out_ref):
        out_ref[:, :width] = x_ref[...]
        out_ref[:, width:] = y_ref[...]

    whole = lambda a: pl.BlockSpec(a.shape, lambda i: (0, 0))
    return pl.pallas_call(
        kernel,
        grid=(1,),
        out_shape=out,
        in_specs=[whole(x), whole(y)],
        out_specs=whole(out),
        cost_estimate=pl.CostEstimate(flops=0, bytes_accessed=2**20, transcendentals=0),
        compiler_params=pltpu.CompilerParams(vmem_limit_bytes=16 * 1024 * 1024),
        name="beside",
    )(x, y)


def follows(x, *others):
    return pl.pallas_call(
        lambda *refs: None,
        out_shape=jax.ShapeDtypeStruct(x.shape, x.dtype),
        in_specs=[pl.BlockSpec(memory_space=pltpu.HBM)] * (1 + len(others)),
        out_specs=pl.BlockSpec(memory_space=pltpu.HBM),
        input_output_aliases={0: 0},
        cost_estimate=pl.CostEstimate(flops=0, bytes_accessed=0, transcendentals=0),
        name="follows",
    )(x, *others)


def swapped(x, by):
    return lax.ppermute(x, "pol", [(i, i ^ by) for i in range(4)])


def on_device(voltages, phase_bin):
    paths = voltages.shape[0]
    time_devs = lax.axis_size("tm")
    path_devs = lax.axis_size("pol")
    total = time_devs * 2 * HALF
    window = jnp.asarray(filter_window())
    twiddle = jnp.asarray(twiddles())
    table = jnp.asarray(inner_table(time_devs))

    me = lax.axis_index("pol")
    src = jnp.arange(4 * LANES, dtype=jnp.int32)[:, None]
    dst = jnp.arange(4 * LANES, dtype=jnp.int32)[None, :]
    device = jnp.bitwise_xor(src // LANES, me)
    target = (src % LANES) // paths * LANES + device * paths + src % paths
    place = (target == dst).astype(jnp.bfloat16)
    own = jnp.asarray(np.eye(LANES).astype(ml_dtypes.bfloat16))
    t_at = lax.axis_index("tm")
    side = t_at // 4 % 2
    order = np.arange(total).reshape(4, 2, 4, 2, HALF)[:, :, :, ::-1].transpose(3, 1, 4, 0, 2)
    order = np.stack([order, order[:, ::-1]]).reshape(2, total)
    pick = (order[:, :, None] == np.arange(total)).astype(np.float32)
    pick = jnp.where(side == 0, jnp.asarray(pick[0]), jnp.asarray(pick[1]))
    labels = jnp.sum(pick * phase_bin.astype(jnp.float32)[None, :], axis=1).astype(jnp.int32)
    number = jnp.arange(total, dtype=jnp.int32)
    ahead = (labels[:, None] == labels[None, :]) & (number[:, None] > number[None, :])
    rank = labels * (total // NBINS) + jnp.sum(ahead.astype(jnp.int32), axis=1)
    rank = jnp.clip(rank, 0, total - 1)
    mask = np.arange(NBINS // 2)[:, None] == np.arange(total // 2)[None, :] // (total // NBINS)
    mask = jnp.asarray(np.repeat(np.tile(mask, (1, 2)), paths, axis=0).astype(ml_dtypes.bfloat16))

    groups = [[y * 8 + z * 4 + x for y in range(4) for x in range(4)] for z in range(2)]
    across = []
    for t in range(time_devs):
        for q in range(path_devs):
            across.append((t * path_devs + q, (t ^ 4) * path_devs + (q ^ 2)))

    def exchanged(x):
        x = x.reshape(time_devs // 2, INNER // time_devs, -1)
        return lax.all_to_all(
            x, "tm", split_axis=0, concat_axis=0, axis_index_groups=groups, tiled=True
        )

    def crossed(x):
        return lax.ppermute(x, ("tm", "pol"), across)

    def after(x, *others):
        return lax.optimization_barrier((x, *others))[0]

    def own_set(x, z):
        return (x, swapped(x, 1), z, swapped(z, 1))

    def cross_set(x, z):
        return (z, swapped(z, 1), x, swapped(x, 1))

    side = side.reshape(1).astype(jnp.int32)
    full = [[(tap, s + tap) for tap in range(TAPS)] for s in range(HALF)]
    part = [[(tap, s + tap - HALF) for tap in range(TAPS) if s + tap >= HALF] for s in range(HALF)]
    carry = [[(tap, s + tap + HALF) for tap in range(TAPS) if s + tap < HALF] for s in range(HALF)]

    wide = RADIX * HALF * paths
    late, late_x = spectra(voltages, window, twiddle, table, side, full, [(0, 0, wide), (1, 0, wide)])
    early, part_x, carry_x = spectra(
        voltages, window, twiddle, table, side, part + carry,
        [(0, 0, 2 * wide), (1, 0, wide), (1, wide, wide)],
    )
    late_x = crossed(late_x)
    part_x = crossed(part_x)
    carry_x = crossed(carry_x)
    late = exchanged(late)
    late_z = swapped(late, 2)
    late_c = swapped(late, 1)
    late_x = exchanged(follows(late_x, late, early))
    late_xz = swapped(late_x, 2)
    late_xc = swapped(late_x, 1)
    late_zc = swapped(late_z, 1)
    early = exchanged(follows(early, late_x, late_z, part_x))
    early_x = exchanged(beside(part_x, carry_x))
    (early,) = joined(early, side, [(0, wide)], late_xz, place, rank)
    early_z = swapped(early, 2)
    low, high = joined(early_x, 1 - side, [(0, wide // 2), (wide // 2, wide // 2)])
    low_z = swapped(low, 2)
    low_c = swapped(low, 1)
    high_c = swapped(high, 1)
    late_xzc = swapped(late_xz, 1)
    early_c = swapped(early, 1)
    early_zc = swapped(early_z, 1)
    common = (late, late_c, late_z, late_zc, late_xz, late_xzc, late_x, late_xc)
    common += (early, early_c, early_z, early_zc)
    high = follows(high, low_z, late_c, late_zc, late_xzc, late_xc, early_c, early_zc, low_c)
    high_z = swapped(high, 2)
    out = grams(common + (low_z, swapped(low_z, 1), low, low_c), place, own, mask, rank, 0, None)
    high_z = follows(high_z, out)
    out = grams(common + (high_z, swapped(high_z, 1), high, high_c), place, own, mask, rank, 1, out)
    return out.reshape(CHANNELS // time_devs, NBINS, 2, paths, paths * path_devs)


def solution(mesh):
    in_specs = (P("pol", "tm"), P())
    out_specs = P("tm", None, None, "pol", None)
    return jax.shard_map(
        on_device, mesh=mesh, in_specs=in_specs, out_specs=out_specs, check_vma=False
    )
```
